32 devices in a mesh: req: 16 (over z, x, core), blk: 2 (over y).
Axes of the slice: x: 2, y: 2, z: 4, core: 2. Of those that a mesh axis runs over, the one named last changes fastest.
Arguments:
- queries: bfloat16 [32, 64, 2048], P('req', 'blk'), may hold values from -5 to 5
- cache_keys: bfloat16 [32, 1024, 2048], P('req', 'blk'), may hold values from -5 to 5
- cache_values: bfloat16 [32, 1024, 2048], P('req', 'blk'), may hold values from -6 to 6
- draft_keys: bfloat16 [32, 64, 2048], P('req', 'blk'), may hold values from -6 to 6
- draft_values: bfloat16 [32, 64, 2048], P('req', 'blk'), may hold values from -6 to 6
- parents: int32 [32, 64], P('req'), may hold values from -1 to 62, as said below
- lengths: int32 [32], P('req'), may hold values from 2 to 1024
- out_weight: bfloat16 [2048, 4096], P('req'), may hold values from -0.125 to 0.125
Outputs:
- mixed: bfloat16 [32, 64, 4096], P('req', 'blk')
The draws below stay inside these ranges and needn't reach their ends.
Inputs may be any that keep to these rules, and one draw needn't show every extreme that they name: parents[r, t] is below t; parents[r, 0] = -1 marks the root, which follows the cache.
All inputs are finite; a program needn't handle non-finite values.
Results may differ from the reference program's by a relative error of at most 0.0054.
Values may be sent and summed in bfloat16 or wider, within the bound.
A program may use at most 128 MiB of HBM per device.

```python
import jax
import jax.numpy as jnp
from jax import lax

D = 4096
HEAD = 128
HEADS = 16
ATT = 2048
TREE = 64
REQS = 32
CACHE = 1024


def joint_fields(key):
    key_q, key_k = jax.random.split(jax.random.fold_in(key, 77), 2)
    query = jnp.clip(jax.random.normal(key_q, (REQS, TREE, ATT), jnp.float32), -5.0, 5.0)
    cache = jnp.clip(jax.random.normal(key_k, (REQS, CACHE, ATT), jnp.float32), -5.0, 5.0)
    return (query, cache)


def draw_queries(key, part):
    return joint_fields(key)[0].astype(jnp.bfloat16)


def draw_cache_keys(key, part):
    return joint_fields(key)[1].astype(jnp.bfloat16)


def draw_parents(key, part):
    index = jnp.arange(TREE, dtype=jnp.int32)[None, :]
    upper = jnp.broadcast_to(jnp.maximum(index, 1), (REQS, TREE))
    picks = jax.random.randint(key, (REQS, TREE), 0, upper, dtype=jnp.int32)
    picks = jnp.where(index == 0, -1, picks)
    picks = jnp.where(index == TREE - 1, TREE - 2, picks)
    return picks.astype(jnp.int32)


def draw_lengths(key, part):
    key_a, key_b = jax.random.split(key)
    first = jax.random.randint(key_a, (REQS,), 2, CACHE + 1, dtype=jnp.int32)
    second = jax.random.randint(key_b, (REQS,), 2, CACHE + 1, dtype=jnp.int32)
    result = jnp.minimum(first, second)
    result = result.at[0].set(CACHE).at[1].set(2)
    return result.astype(jnp.int32)


def shard_levels(key, shape, pieces, smallest, top_value):
    def one(axis_at, shards_of):
        draws = jax.random.uniform(jax.random.fold_in(jax.random.fold_in(key, 6), axis_at), (shards_of,), jnp.float32, smallest / len(pieces), top_value / len(pieces))
        return jnp.repeat(jnp.exp(draws), shape[axis_at] // shards_of).reshape((-1,) + (1,) * (len(shape) - axis_at - 1))

    loudness = one(*pieces[0])
    for cut in pieces[1:]:
        loudness = loudness * one(*cut)
    return loudness


def bell_draw(key, shape, deviation, reach, cuts=(), kind=jnp.bfloat16):
    entries = deviation * jax.random.normal(key, shape, jnp.float32)
    if cuts:
        entries = entries * shard_levels(key, shape, cuts, -0.22, 0.18)
    return jnp.clip(entries, -reach, reach).astype(kind)


def setup_inputs(seed: int = 0) -> dict:
    key_list = jax.random.split(jax.random.key(seed), 9)
    queries = draw_queries(jax.random.fold_in(key_list[8], 71), 0)
    cache_keys = draw_cache_keys(jax.random.fold_in(key_list[8], 71), 0)
    cache_values = bell_draw(key_list[2], (REQS, CACHE, ATT), 1.0, 6.0, ((0, 16), (1, 2)))
    draft_keys = bell_draw(key_list[3], (REQS, TREE, ATT), 1.0, 6.0, ((0, 16), (1, 2)))
    draft_values = bell_draw(key_list[4], (REQS, TREE, ATT), 1.0, 6.0, ((0, 16), (1, 2)))
    parents = draw_parents(jax.random.fold_in(key_list[8], 71), 0)
    lengths = draw_lengths(jax.random.fold_in(key_list[8], 71), 0)
    out_weight = bell_draw(key_list[7], (ATT, D), ATT ** -0.5, 0.125, ((0, 16),))
    return {"queries": queries, "cache_keys": cache_keys, "cache_values": cache_values, "draft_keys": draft_keys, "draft_values": draft_values, "parents": parents, "lengths": lengths, "out_weight": out_weight}


def ancestors(parent_row):
    index = jnp.arange(TREE)
    links = (parent_row[:, None] == index[None, :]).astype(jnp.float32)
    links = links + (index[:, None] == index[None, :]).astype(jnp.float32)
    for _ in range(TREE.bit_length()):
        links = jnp.minimum(jnp.dot(links, links, precision=lax.Precision.HIGHEST, preferred_element_type=jnp.float32), 1.0)
    return links > 0.5


def one_request(items):
    query, cache_k, cache_v, draft_k, draft_v, parent_row, length = items
    scale = HEAD ** -0.5
    qf = query.astype(jnp.float32).reshape(TREE, HEADS, HEAD)
    keys = jnp.concatenate([cache_k, draft_k], axis=0).astype(jnp.float32).reshape(-1, HEADS, HEAD)
    values = jnp.concatenate([cache_v, draft_v], axis=0).astype(jnp.float32).reshape(-1, HEADS, HEAD)
    scores = jnp.einsum("the,khe->htk", qf, keys) * scale
    cache_seen = jnp.broadcast_to((jnp.arange(CACHE) < length)[None, :], (TREE, CACHE))
    seen = jnp.concatenate([cache_seen, ancestors(parent_row)], axis=1)[None]
    scores = jnp.where(seen, scores, -1e30)
    row_max = jnp.max(scores, axis=-1)
    weights = jnp.where(seen, jnp.exp(scores - row_max[..., None]), 0.0)
    totals = jnp.sum(weights, axis=-1)
    rounded = lax.optimization_barrier(weights.astype(jnp.bfloat16)).astype(jnp.float32)
    numer = jnp.einsum("htk,khe->the", rounded, values)
    attended = numer / jnp.transpose(totals)[..., None]
    return attended.reshape(TREE, ATT).astype(jnp.bfloat16)


def reference(queries, cache_keys, cache_values, draft_keys, draft_values, parents, lengths, out_weight):
    attended = lax.map(one_request, (queries, cache_keys, cache_values, draft_keys, draft_values, parents, lengths))
    mixed = jnp.dot(attended.reshape(-1, ATT), out_weight, preferred_element_type=jnp.float32)
    return mixed.astype(jnp.bfloat16).reshape(REQS, TREE, D)
```

```python
import functools

import jax
import jax.numpy as jnp
from jax import lax
from jax.experimental import pallas as pl
from jax.experimental.pallas import tpu as pltpu
from jax.sharding import PartitionSpec as P

HEAD = 128
HEADS = 16
LOW = 4
PARTS = 4
EXCH = 2
CHUNK = 256
MESH = pl.DeviceIdType.MESH
NEG = -1e30
COEF = HEAD**-0.5 * 1.4426950408889634


def flip(value, bits):
    out = value
    bit = 1
    while bit <= bits:
        if bits & bit:
            out = out + bit - 2 * bit * ((value // bit) % 2)
        bit *= 2
    return out


def kernel(
    nreq, nblk,
    q_hbm, ck_hbm, cv_hbm, dk_hbm, dv_hbm, par_ref, len_ref, w_hbm,
    out_hbm,
    qbuf, kbuf, vbuf, dkbuf, dvbuf, vis, nsend, nrecv, ssend, srecv, abuf, wbuf, obuf,
    kv_sem, d_sem, q_send, q_recv, n_send, n_recv, s_send, s_recv,
    wz_send, wx_send, wc_send, w_recv, a_send, a_recv, o_send, o_recv,
):
    batch, own, width = q_hbm.shape
    keys = ck_hbm.shape[1]
    tree = own * nblk
    rows_w, model = w_hbm.shape
    group = 2 * nblk
    ncols = model // group
    depth = nreq // LOW
    req, blk = lax.axis_index("req"), lax.axis_index("blk")
    z, x, c = req // LOW, (req // 2) % 2, req % 2

    def at(zz, xx, cc):
        return zz * LOW + xx * 2 + cc

    part = width // PARTS
    pcols = [pl.ds(p * part, part) for p in range(PARTS)]
    xwidth = width // EXCH
    ecols = [pl.ds(e * xwidth, xwidth) for e in range(EXCH)]

    locals_d = [
        pltpu.make_async_copy(q_hbm, qbuf.at[blk], d_sem.at[0]),
        pltpu.make_async_copy(dk_hbm, dkbuf, d_sem.at[1]),
        pltpu.make_async_copy(dv_hbm, dvbuf, d_sem.at[2]),
    ]
    for copy in locals_d:
        copy.start()
    kv = []
    for p in range(PARTS):
        pair = (
            pltpu.make_async_copy(ck_hbm.at[:, :, pcols[p]], kbuf.at[:, :, pcols[p]], kv_sem.at[0, p]),
            pltpu.make_async_copy(cv_hbm.at[:, :, pcols[p]], vbuf.at[:, :, pcols[p]], kv_sem.at[1, p]),
        )
        for copy in pair:
            copy.start()
        kv.append(pair)

    xpeer, cpeer = at(z, 1 - x, c), at(z, x, 1 - c)
    members = [
        (flip(z, a), lax.rem(blk + b, nblk)) for a in range(2) for b in range(nblk) if a or b
    ]
    peers = [(at(flip(z, d), x, c), blk) for d in range(1, depth)] + [(xpeer, blk), (cpeer, blk)]
    peers += [
        (at(flip(z, a), x, c), lax.rem(blk + b, nblk)) for a in range(2) for b in range(1, nblk)
    ]
    barrier = pltpu.get_barrier_semaphore()
    for peer in peers:
        pl.semaphore_signal(barrier, inc=1, device_id=peer, device_id_type=MESH)
    pl.semaphore_wait(barrier, len(peers))

    def remote(src, dst, send, recv, peer):
        return pltpu.make_async_remote_copy(
            src_ref=src, dst_ref=dst, send_sem=send, recv_sem=recv, device_id=peer, device_id_type=MESH
        )

    sent = []

    def send(*what):
        copy = remote(*what)
        copy.start()
        sent.append(copy)

    def await_recv(dst, sem):
        remote(dst, dst, wz_send.at[0], sem, (xpeer, blk)).wait_recv()

    for b in range(1, nblk):
        send(q_hbm, qbuf.at[blk], q_send.at[b], q_recv.at[blk], (req, lax.rem(blk + b, nblk)))

    def wrows(source):
        return wbuf.at[pl.ds(pl.multiple_of(source * rows_w, rows_w), rows_w)]

    def wsrc(zz):
        index = (zz % 2) * nblk + blk
        return w_hbm.at[:, pl.ds(pl.multiple_of(index * ncols, ncols), ncols)]

    for d in range(1, depth):
        zz = flip(z, d)
        send(wsrc(zz), wrows(req), wz_send.at[d], w_recv.at[req], (at(zz, x, c), blk))
    send(wsrc(z), wrows(req), wx_send.at[0], w_recv.at[req], (xpeer, blk))
    send(wsrc(z), wrows(req), wc_send.at[0], w_recv.at[req], (cpeer, blk))
    own_w = pltpu.make_async_copy(wsrc(z), wrows(req), w_recv.at[req])
    own_w.start()

    def forward_z(d):
        source = at(flip(z, d), x, c)
        await_recv(wrows(source), w_recv.at[source])
        send(wrows(source), wrows(source), wx_send.at[d], w_recv.at[source], (xpeer, blk))
        send(wrows(source), wrows(source), wc_send.at[d], w_recv.at[source], (cpeer, blk))

    def forward_x(d):
        source = at(flip(z, d), 1 - x, c)
        await_recv(wrows(source), w_recv.at[source])
        send(wrows(source), wrows(source), wc_send.at[depth + d], w_recv.at[source], (cpeer, blk))

    row_i = lax.broadcasted_iota(jnp.int32, (tree, tree), 0)
    col_i = lax.broadcasted_iota(jnp.int32, (tree, tree), 1)
    pick = (
        lax.broadcasted_iota(jnp.int32, (tree, own), 0)
        == lax.broadcasted_iota(jnp.int32, (tree, own), 1) + blk * own
    ).astype(jnp.float32).astype(jnp.bfloat16)
    for r in range(batch):
        links = ((par_ref[pl.ds(r, 1), :] == row_i) | (row_i == col_i)).astype(jnp.float32)
        for _ in range((tree - 1).bit_length()):
            half = links.astype(jnp.bfloat16)
            links = jnp.minimum(jnp.dot(half, half, preferred_element_type=jnp.float32), 1.0)
        vis[r] = lax.dot_general(
            links.astype(jnp.bfloat16), pick, (((0,), (0,)), ((), ())),
            preferred_element_type=jnp.float32,
        )
    ssend[...] = jnp.zeros_like(ssend)

    slot = lax.broadcasted_iota(jnp.int32, (1, keys), 1) + blk * keys
    seen = [slot < len_ref[r] for r in range(batch)]
    lane = lax.broadcasted_iota(jnp.int32, (batch * own, 128), 1)
    per_e = HEADS // EXCH

    def head(e, h):
        cols = pl.ds(pl.multiple_of(h * HEAD, HEAD), HEAD)
        stats = []
        for r in range(batch):
            pieces = [qbuf[b, r, :, cols] for b in range(nblk)]
            if own % 16:
                q = jnp.concatenate([piece.astype(jnp.float32) for piece in pieces], axis=0)
                q = q.astype(jnp.bfloat16)
            else:
                q = jnp.concatenate(pieces, axis=0)
            dims = (((1,), (1,)), ((), ()))
            s1 = lax.dot_general(q, kbuf[r, :, cols], dims, preferred_element_type=jnp.float32)
            s2 = lax.dot_general(q, dkbuf[r, :, cols], dims, preferred_element_type=jnp.float32)
            s1 = jnp.where(seen[r], s1, NEG)
            s2 = jnp.where(vis[r] > 0.5, s2, NEG)
            top = jnp.maximum(
                jnp.max(s1, axis=-1, keepdims=True), jnp.max(s2, axis=-1, keepdims=True)
            )
            top = jnp.maximum(top, 0.1 * NEG)
            p1 = jnp.exp2((s1 - top) * COEF)
            p2 = jnp.exp2((s2 - top) * COEF)
            total = jnp.sum(p1, axis=-1, keepdims=True) + jnp.sum(p2, axis=-1, keepdims=True)
            numer = jnp.dot(
                p1.astype(jnp.bfloat16), vbuf[r, :, cols], preferred_element_type=jnp.float32
            ) + jnp.dot(
                p2.astype(jnp.bfloat16), dvbuf[r, :, cols], preferred_element_type=jnp.float32
            )
            stats.append((top, total, numer))
        at_lane = h - e * per_e
        for b in range(nblk):
            rows = slice(b * own, (b + 1) * own)
            top, total, numer = (
                jnp.concatenate([s[i][rows] for s in stats], axis=0) for i in range(3)
            )
            nsend[b, :, cols] = numer.astype(jnp.bfloat16)
            ssend[e, b] = jnp.where(
                lane == at_lane, top, jnp.where(lane == at_lane + 64, total, ssend[e, b])
            )

    def attend(p):
        for copy in kv[p]:
            copy.wait()
        count = HEADS // PARTS
        e = p * EXCH // PARTS

        def body(i, carry):
            head(e, p * count + 2 * i)
            head(e, p * count + 2 * i + 1)
            return carry

        lax.fori_loop(0, count // 2, body, 0)

    def exchange(e):
        for b in range(1, nblk):
            to = lax.rem(blk + b, nblk)
            send(nsend.at[to, :, ecols[e]], nrecv.at[blk, :, ecols[e]], n_send.at[e, b], n_recv.at[e, blk], (req, to))
            send(ssend.at[e, to], srecv.at[e, blk], s_send.at[e, b], s_recv.at[e, blk], (req, to))

    mine = (z % 2) * nblk + blk

    def merge(e):
        stats = [ssend[e, blk]]
        froms = [blk]
        for b in range(1, nblk):
            source = lax.rem(blk + b, nblk)
            await_recv(nrecv.at[source, :, ecols[e]], n_recv.at[e, source])
            await_recv(srecv.at[e, source], s_recv.at[e, source])
            stats.append(srecv[e, source])
            froms.append(source)
        top = functools.reduce(jnp.maximum, stats)
        factors = [jnp.exp2(jnp.minimum((s - top) * COEF, 0.0)) for s in stats]
        total = sum(pltpu.roll(s, 64, 1) * f for s, f in zip(stats, factors))
        factors = [f / total for f in factors]
        for i in range(per_e):
            cols = pl.ds((e * per_e + i) * HEAD, HEAD)
            row = nsend[blk, :, cols].astype(jnp.float32) * factors[0][:, i : i + 1]
            for source, f in zip(froms[1:], factors[1:]):
                row = row + nrecv[source, :, cols].astype(jnp.float32) * f[:, i : i + 1]
            abuf[mine, :, cols] = row.astype(jnp.bfloat16)
        for j, (zz, yy) in enumerate(members):
            block = abuf.at[mine, :, ecols[e]]
            send(block, block, a_send.at[e, j], a_recv.at[e, mine], (at(zz, x, c), yy))

    for copy in locals_d:
        copy.wait()
    for b in range(1, nblk):
        source = lax.rem(blk + b, nblk)
        await_recv(qbuf.at[source], q_recv.at[source])

    attend(0)
    attend(1)
    exchange(0)
    forward_z(1)
    attend(2)
    forward_x(0)
    merge(0)
    forward_z(2)
    attend(3)
    exchange(1)
    forward_x(1)
    for d in range(3, depth):
        forward_z(d)
    merge(1)
    for d in range(2, depth):
        forward_x(d)

    own_w.wait()
    for source in range(depth):
        for low in ((x, 1 - c), (1 - x, 1 - c)):
            index = at(flip(z, source), *low)
            await_recv(wrows(index), w_recv.at[index])
    for e in range(EXCH):
        for zz, yy in members:
            index = (zz % 2) * nblk + yy
            await_recv(abuf.at[index, :, ecols[e]], a_recv.at[e, index])

    homes = []
    for n in range(ncols // CHUNK):
        cols = pl.ds(n * CHUNK, CHUNK)
        mixed = jnp.dot(
            abuf[...].reshape(group * batch * own, width), wbuf[:, cols],
            preferred_element_type=jnp.float32,
        )
        obuf[:, :, :, cols] = mixed.reshape(group, batch, own, CHUNK).astype(jnp.bfloat16)
        there = pl.ds(pl.multiple_of(mine * ncols + n * CHUNK, CHUNK), CHUNK)
        for j, (zz, yy) in enumerate(members):
            index = (zz % 2) * nblk + yy
            send(
                obuf.at[index, :, :, cols], out_hbm.at[:, :, there],
                o_send.at[n, j], o_recv.at[n, mine], (at(zz, x, c), yy),
            )
        home = pltpu.make_async_copy(obuf.at[mine, :, :, cols], out_hbm.at[:, :, there], o_recv.at[n, mine])
        home.start()
        homes.append(home)
    for n in range(ncols // CHUNK):
        homes[n].wait()
        for zz, yy in members:
            index = (zz % 2) * nblk + yy
            there = pl.ds(pl.multiple_of(index * ncols + n * CHUNK, CHUNK), CHUNK)
            await_recv(out_hbm.at[:, :, there], o_recv.at[n, index])
    for copy in sent:
        copy.wait_send()


def shards(nreq, nblk, queries, cache_keys, cache_values, draft_keys, draft_values, parents, lengths, out_weight):
    batch, own, width = queries.shape
    keys = cache_keys.shape[1]
    tree = own * nblk
    rows_w, model = out_weight.shape
    group = 2 * nblk
    ncols = model // group
    depth = nreq // LOW
    bf16, f32 = jnp.bfloat16, jnp.float32
    dma = pltpu.SemaphoreType.DMA
    hbm = pl.BlockSpec(memory_space=pltpu.HBM)
    vmem = pl.BlockSpec(memory_space=pltpu.VMEM)
    smem = pl.BlockSpec(memory_space=pltpu.SMEM)
    pieces = ncols // CHUNK
    return pl.pallas_call(
        functools.partial(kernel, nreq, nblk),
        out_shape=jax.ShapeDtypeStruct((batch, own, model), bf16),
        in_specs=[hbm, hbm, hbm, hbm, hbm, vmem, smem, hbm],
        out_specs=hbm,
        scratch_shapes=[
            pltpu.VMEM((nblk, batch, own, width), bf16),
            pltpu.VMEM((batch, keys, width), bf16),
            pltpu.VMEM((batch, keys, width), bf16),
            pltpu.VMEM((batch, own, width), bf16),
            pltpu.VMEM((batch, own, width), bf16),
            pltpu.VMEM((batch, tree, own), f32),
            pltpu.VMEM((nblk, batch * own, width), bf16),
            pltpu.VMEM((nblk, batch * own, width), bf16),
            pltpu.VMEM((EXCH, nblk, batch * own, 128), f32),
            pltpu.VMEM((EXCH, nblk, batch * own, 128), f32),
            pltpu.VMEM((group, batch * own, width), bf16),
            pltpu.VMEM((rows_w * nreq, ncols), bf16),
            pltpu.VMEM((group, batch, own, ncols), bf16),
            dma((2, PARTS)),
            dma((3,)),
            dma((nblk,)),
            dma((nblk,)),
            dma((EXCH, nblk)),
            dma((EXCH, nblk)),
            dma((EXCH, nblk)),
            dma((EXCH, nblk)),
            dma((depth,)),
            dma((depth,)),
            dma((2 * depth,)),
            dma((nreq,)),
            dma((EXCH, group)),
            dma((EXCH, group)),
            dma((pieces, group)),
            dma((pieces, group)),
        ],
        compiler_params=pltpu.CompilerParams(
            collective_id=0, has_side_effects=True, vmem_limit_bytes=50 * 1024 * 1024
        ),
    )(queries, cache_keys, cache_values, draft_keys, draft_values, parents, lengths, out_weight)


def solution(mesh):
    in_specs = (
        P("req", "blk", None),
        P("req", "blk", None),
        P("req", "blk", None),
        P("req", "blk", None),
        P("req", "blk", None),
        P("req", None),
        P("req"),
        P("req", None),
    )
    out_specs = P("req", "blk", None)
    body = functools.partial(shards, mesh.shape["req"], mesh.shape["blk"])
    return jax.shard_map(body, mesh=mesh, in_specs=in_specs, out_specs=out_specs, check_vma=False)
```

```python
import functools

import jax
import jax.numpy as jnp
from jax import lax
from jax.experimental import pallas as pl
from jax.experimental.pallas import tpu as pltpu
from jax.sharding import PartitionSpec as P

HEAD = 128
HEADS = 16
LOW = 4
PARTS = 4
CHUNK = 256
MESH = pl.DeviceIdType.MESH
NEG = -1e30
COEF = HEAD**-0.5 * 1.4426950408889634


def flip(value, bits):
    out = value
    bit = 1
    while bit <= bits:
        if bits & bit:
            out = out + bit - 2 * bit * ((value // bit) % 2)
        bit *= 2
    return out


def kernel(
    nreq, nblk,
    q_hbm, ck_hbm, cv_hbm, dk_hbm, dv_hbm, par_ref, len_ref, w_hbm,
    out_hbm,
    qbuf, kbuf, vbuf, dkbuf, dvbuf, vis, nsend, nrecv, stat, ssend, srecv, abuf, wbuf, obuf,
    kv_sem, d_sem, q_send, q_recv, n_send, n_recv, s_send, s_recv,
    wz_send, wx_send, wc_send, w_recv, a_send, a_recv, o_send, o_recv,
):
    batch, own, width = q_hbm.shape
    keys = ck_hbm.shape[1]
    tree = own * nblk
    rows_w, model = w_hbm.shape
    group = 2 * nblk
    ncols = model // group
    depth = nreq // LOW
    req, blk = lax.axis_index("req"), lax.axis_index("blk")
    z, x, c = req // LOW, (req // 2) % 2, req % 2

    def at(zz, xx, cc):
        return zz * LOW + xx * 2 + cc

    part = width // PARTS
    pcols = [pl.ds(p * part, part) for p in range(PARTS)]

    locals_d = [
        pltpu.make_async_copy(q_hbm, qbuf.at[blk], d_sem.at[0]),
        pltpu.make_async_copy(dk_hbm, dkbuf, d_sem.at[1]),
        pltpu.make_async_copy(dv_hbm, dvbuf, d_sem.at[2]),
    ]
    for copy in locals_d:
        copy.start()
    kv = []
    for p in range(PARTS):
        pair = (
            pltpu.make_async_copy(ck_hbm.at[:, :, pcols[p]], kbuf.at[:, :, pcols[p]], kv_sem.at[0, p]),
            pltpu.make_async_copy(cv_hbm.at[:, :, pcols[p]], vbuf.at[:, :, pcols[p]], kv_sem.at[1, p]),
        )
        for copy in pair:
            copy.start()
        kv.append(pair)

    xpeer, cpeer = at(z, 1 - x, c), at(z, x, 1 - c)
    members = [
        (flip(z, a), lax.rem(blk + b, nblk)) for a in range(2) for b in range(nblk) if a or b
    ]
    peers = [(at(flip(z, d), x, c), blk) for d in range(1, depth)] + [(xpeer, blk), (cpeer, blk)]
    peers += [
        (at(flip(z, a), x, c), lax.rem(blk + b, nblk)) for a in range(2) for b in range(1, nblk)
    ]
    barrier = pltpu.get_barrier_semaphore()
    for peer in peers:
        pl.semaphore_signal(barrier, inc=1, device_id=peer, device_id_type=MESH)
    pl.semaphore_wait(barrier, len(peers))

    def remote(src, dst, send, recv, peer):
        return pltpu.make_async_remote_copy(
            src_ref=src, dst_ref=dst, send_sem=send, recv_sem=recv, device_id=peer, device_id_type=MESH
        )

    sent = []

    def send(*what):
        copy = remote(*what)
        copy.start()
        sent.append(copy)

    def await_recv(dst, sem):
        remote(dst, dst, wz_send.at[0], sem, (xpeer, blk)).wait_recv()

    for p in range(PARTS):
        for b in range(1, nblk):
            send(
                q_hbm.at[:, :, pcols[p]], qbuf.at[blk, :, :, pcols[p]],
                q_send.at[p, b], q_recv.at[p, blk], (req, lax.rem(blk + b, nblk)),
            )

    def wrows(source):
        return wbuf.at[pl.ds(pl.multiple_of(source * rows_w, rows_w), rows_w)]

    def wsrc(zz):
        index = (zz % 2) * nblk + blk
        return w_hbm.at[:, pl.ds(pl.multiple_of(index * ncols, ncols), ncols)]

    for d in range(1, depth):
        zz = flip(z, d)
        send(wsrc(zz), wrows(req), wz_send.at[d], w_recv.at[req], (at(zz, x, c), blk))
    send(wsrc(z), wrows(req), wx_send.at[0], w_recv.at[req], (xpeer, blk))
    send(wsrc(z), wrows(req), wc_send.at[0], w_recv.at[req], (cpeer, blk))
    own_w = pltpu.make_async_copy(wsrc(z), wrows(req), w_recv.at[req])
    own_w.start()

    def forward_z(d):
        source = at(flip(z, d), x, c)
        await_recv(wrows(source), w_recv.at[source])
        send(wrows(source), wrows(source), wx_send.at[d], w_recv.at[source], (xpeer, blk))
        send(wrows(source), wrows(source), wc_send.at[d], w_recv.at[source], (cpeer, blk))

    def forward_x(d):
        source = at(flip(z, d), 1 - x, c)
        await_recv(wrows(source), w_recv.at[source])
        send(wrows(source), wrows(source), wc_send.at[depth + d], w_recv.at[source], (cpeer, blk))

    row_i = lax.broadcasted_iota(jnp.int32, (tree, tree), 0)
    col_i = lax.broadcasted_iota(jnp.int32, (tree, tree), 1)
    pick = (
        lax.broadcasted_iota(jnp.int32, (tree, own), 0)
        == lax.broadcasted_iota(jnp.int32, (tree, own), 1) + blk * own
    ).astype(jnp.float32).astype(jnp.bfloat16)
    for r in range(batch):
        links = ((par_ref[pl.ds(r, 1), :] == row_i) | (row_i == col_i)).astype(jnp.float32)
        for _ in range((tree - 1).bit_length()):
            half = links.astype(jnp.bfloat16)
            links = jnp.minimum(jnp.dot(half, half, preferred_element_type=jnp.float32), 1.0)
        vis[r] = lax.dot_general(
            links.astype(jnp.bfloat16), pick, (((0,), (0,)), ((), ())),
            preferred_element_type=jnp.float32,
        )
    stat[...] = jnp.zeros_like(stat)

    slot = lax.broadcasted_iota(jnp.int32, (1, keys), 1) + blk * keys
    seen = [slot < len_ref[r] for r in range(batch)]
    lane = lax.broadcasted_iota(jnp.int32, (batch * own, 128), 1)
    per_p = HEADS // PARTS

    def head(p, h):
        cols = pl.ds(pl.multiple_of(h * HEAD, HEAD), HEAD)
        stats = []
        for r in range(batch):
            pieces = [qbuf[b, r, :, cols] for b in range(nblk)]
            if own % 16:
                q = jnp.concatenate([piece.astype(jnp.float32) for piece in pieces], axis=0)
                q = q.astype(jnp.bfloat16)
            else:
                q = jnp.concatenate(pieces, axis=0)
            dims = (((1,), (1,)), ((), ()))
            s1 = lax.dot_general(q, kbuf[r, :, cols], dims, preferred_element_type=jnp.float32)
            s2 = lax.dot_general(q, dkbuf[r, :, cols], dims, preferred_element_type=jnp.float32)
            s1 = jnp.where(seen[r], s1, NEG)
            s2 = jnp.where(vis[r] > 0.5, s2, NEG)
            top = jnp.maximum(
                jnp.max(s1, axis=-1, keepdims=True), jnp.max(s2, axis=-1, keepdims=True)
            )
            top = jnp.maximum(top, 0.1 * NEG)
            p1 = jnp.exp2((s1 - top) * COEF)
            p2 = jnp.exp2((s2 - top) * COEF)
            total = jnp.sum(p1, axis=-1, keepdims=True) + jnp.sum(p2, axis=-1, keepdims=True)
            numer = jnp.dot(
                p1.astype(jnp.bfloat16), vbuf[r, :, cols], preferred_element_type=jnp.float32
            ) + jnp.dot(
                p2.astype(jnp.bfloat16), dvbuf[r, :, cols], preferred_element_type=jnp.float32
            )
            stats.append((top, total, numer))
        at_lane = h - p * per_p
        for b in range(nblk):
            rows = slice(b * own, (b + 1) * own)
            top, total, numer = (
                jnp.concatenate([s[i][rows] for s in stats], axis=0) for i in range(3)
            )
            nsend[b, :, cols] = numer.astype(jnp.bfloat16)
            at_rows = pl.ds(b * batch * own, batch * own)
            stat[p, at_rows] = jnp.where(
                lane == at_lane, top, jnp.where(lane == at_lane + per_p, total, stat[p, at_rows])
            )

    def attend(p):
        for copy in kv[p]:
            copy.wait()
        for b in range(1, nblk):
            source = lax.rem(blk + b, nblk)
            await_recv(qbuf.at[source, :, :, pcols[p]], q_recv.at[p, source])

        def body(i, carry):
            head(p, p * per_p + 2 * i)
            head(p, p * per_p + 2 * i + 1)
            return carry

        lax.fori_loop(0, per_p // 2, body, 0)

    def exchange(p):
        ssend[p] = stat[p].T[: 2 * per_p]
        for b in range(1, nblk):
            to = (req, lax.rem(blk + b, nblk))
            send(
                nsend.at[:, :, pcols[p]], nrecv.at[blk, :, :, pcols[p]],
                n_send.at[p, b], n_recv.at[p, blk], to,
            )
            send(ssend.at[p], srecv.at[p, blk], s_send.at[p, b], s_recv.at[p, blk], to)

    zmod = z % 2
    mine = zmod * nblk + blk
    zpeer = (at(flip(z, 1), x, c), blk)

    def tokens(of):
        return abuf.at[pl.ds(of * nblk, nblk)]

    def merge(p):
        stats = [stat[p][:, : 2 * per_p]]
        for b in range(1, nblk):
            source = lax.rem(blk + b, nblk)
            await_recv(nrecv.at[source, :, :, pcols[p]], n_recv.at[p, source])
            await_recv(srecv.at[p, source], s_recv.at[p, source])
            stats.append(srecv[p, source].T)
        tops = [s[:, :per_p] for s in stats]
        sums = [s[:, per_p:] for s in stats]
        top = functools.reduce(jnp.maximum, tops)
        factors = [jnp.exp2((t - top) * COEF) for t in tops]
        total = sum(s * f for s, f in zip(sums, factors))
        factors = [f / total for f in factors]
        for b in range(nblk):
            rows = slice(b * batch * own, (b + 1) * batch * own)
            for i in range(per_p):
                cols = pl.ds((p * per_p + i) * HEAD, HEAD)
                row = nsend[b, :, cols].astype(jnp.float32) * factors[0][rows, i : i + 1]
                for a in range(1, nblk):
                    piece = nrecv[lax.rem(blk + a, nblk), b, :, cols].astype(jnp.float32)
                    row = row + piece * factors[a][rows, i : i + 1]
                abuf[zmod * nblk + b, :, cols] = row.astype(jnp.bfloat16)
        block = tokens(zmod).at[:, :, pcols[p]]
        send(block, block, a_send.at[p], a_recv.at[p], zpeer)

    for copy in locals_d:
        copy.wait()

    attend(0)
    exchange(0)
    attend(1)
    exchange(1)
    forward_z(1)
    forward_x(0)
    merge(0)
    attend(2)
    exchange(2)
    forward_z(2)
    forward_x(1)
    merge(1)
    attend(3)
    exchange(3)
    for d in range(3, depth):
        forward_z(d)
    merge(2)
    merge(3)
    for d in range(2, depth):
        forward_x(d)

    own_w.wait()
    for source in range(depth):
        for low in ((x, 1 - c), (1 - x, 1 - c)):
            index = at(flip(z, source), *low)
            await_recv(wrows(index), w_recv.at[index])
    for p in range(PARTS):
        await_recv(tokens(1 - zmod).at[:, :, pcols[p]], a_recv.at[p])

    homes = []
    for n in range(ncols // CHUNK):
        cols = pl.ds(n * CHUNK, CHUNK)
        mixed = jnp.dot(
            abuf[...].reshape(group * batch * own, width), wbuf[:, cols],
            preferred_element_type=jnp.float32,
        )
        obuf[:, :, :, cols] = mixed.reshape(group, batch, own, CHUNK).astype(jnp.bfloat16)
        there = pl.ds(pl.multiple_of(mine * ncols + n * CHUNK, CHUNK), CHUNK)
        for j, (zz, yy) in enumerate(members):
            index = (zz % 2) * nblk + yy
            send(
                obuf.at[index, :, :, cols], out_hbm.at[:, :, there],
                o_send.at[n, j], o_recv.at[n, mine], (at(zz, x, c), yy),
            )
        home = pltpu.make_async_copy(obuf.at[mine, :, :, cols], out_hbm.at[:, :, there], o_recv.at[n, mine])
        home.start()
        homes.append(home)
    for n in range(ncols // CHUNK):
        homes[n].wait()
        for zz, yy in members:
            index = (zz % 2) * nblk + yy
            there = pl.ds(pl.multiple_of(index * ncols + n * CHUNK, CHUNK), CHUNK)
            await_recv(out_hbm.at[:, :, there], o_recv.at[n, index])
    for copy in sent:
        copy.wait_send()


def shards(nreq, nblk, queries, cache_keys, cache_values, draft_keys, draft_values, parents, lengths, out_weight):
    batch, own, width = queries.shape
    keys = cache_keys.shape[1]
    tree = own * nblk
    rows_w, model = out_weight.shape
    group = 2 * nblk
    ncols = model // group
    depth = nreq // LOW
    bf16, f32 = jnp.bfloat16, jnp.float32
    dma = pltpu.SemaphoreType.DMA
    hbm = pl.BlockSpec(memory_space=pltpu.HBM)
    vmem = pl.BlockSpec(memory_space=pltpu.VMEM)
    smem = pl.BlockSpec(memory_space=pltpu.SMEM)
    pieces = ncols // CHUNK
    return pl.pallas_call(
        functools.partial(kernel, nreq, nblk),
        out_shape=jax.ShapeDtypeStruct((batch, own, model), bf16),
        in_specs=[hbm, hbm, hbm, hbm, hbm, vmem, smem, hbm],
        out_specs=hbm,
        scratch_shapes=[
            pltpu.VMEM((nblk, batch, own, width), bf16),
            pltpu.VMEM((batch, keys, width), bf16),
            pltpu.VMEM((batch, keys, width), bf16),
            pltpu.VMEM((batch, own, width), bf16),
            pltpu.VMEM((batch, own, width), bf16),
            pltpu.VMEM((batch, tree, own), f32),
            pltpu.VMEM((nblk, batch * own, width), bf16),
            pltpu.VMEM((nblk, nblk, batch * own, width), bf16),
            pltpu.VMEM((PARTS, batch * tree, 128), f32),
            pltpu.VMEM((PARTS, 2 * HEADS // PARTS, batch * tree), f32),
            pltpu.VMEM((PARTS, nblk, 2 * HEADS // PARTS, batch * tree), f32),
            pltpu.VMEM((group, batch * own, width), bf16),
            pltpu.VMEM((rows_w * nreq, ncols), bf16),
            pltpu.VMEM((group, batch, own, ncols), bf16),
            dma((2, PARTS)),
            dma((3,)),
            dma((PARTS, nblk)),
            dma((PARTS, nblk)),
            dma((PARTS, nblk)),
            dma((PARTS, nblk)),
            dma((PARTS, nblk)),
            dma((PARTS, nblk)),
            dma((depth,)),
            dma((depth,)),
            dma((2 * depth,)),
            dma((nreq,)),
            dma((PARTS,)),
            dma((PARTS,)),
            dma((pieces, group)),
            dma((pieces, group)),
        ],
        compiler_params=pltpu.CompilerParams(
            collective_id=0, has_side_effects=True, vmem_limit_bytes=58 * 1024 * 1024
        ),
    )(queries, cache_keys, cache_values, draft_keys, draft_values, parents, lengths, out_weight)


def solution(mesh):
    in_specs = (
        P("req", "blk", None),
        P("req", "blk", None),
        P("req", "blk", None),
        P("req", "blk", None),
        P("req", "blk", None),
        P("req", None),
        P("req"),
        P("req", None),
    )
    out_specs = P("req", "blk", None)
    body = functools.partial(shards, mesh.shape["req"], mesh.shape["blk"])
    return jax.shard_map(body, mesh=mesh, in_specs=in_specs, out_specs=out_specs, check_vma=False)
```
